128 devices in a mesh: fsdp: 8 (over x_lo, z), ctx: 16 (over x_hi, y, core).
Axes of the slice: x: 4 (x_hi: 2, x_lo: 2; x = x_hi * 2 + x_lo), y: 4, z: 4, core: 2. Of those that a mesh axis runs over, the one named last changes fastest.
Arguments:
- streams: bfloat16 [8, 4096, 12288], P('fsdp', 'ctx'), may hold values from -6 to 6
- cotangent: bfloat16 [8, 4096, 4096], P('fsdp', 'ctx'), may hold values from -6 to 6
- filters: float32 [256, 128], P(('fsdp', 'ctx')), may hold values from -0.54 to 0.54
- short_taps: float32 [3, 12288], P(None, ('fsdp', 'ctx')), may hold values from -3.6 to 3.6
Outputs:
- result: bfloat16 [8, 4096, 4096], P('fsdp', 'ctx')
- stream_grad: bfloat16 [8, 4096, 12288], P('fsdp', 'ctx')
- filter_grad: float32 [256, 128], P(('fsdp', 'ctx'))
- short_grad: float32 [3, 12288], P(None, ('fsdp', 'ctx'))
The draws below stay inside these ranges and needn't reach their ends.
All inputs are finite; a program needn't handle non-finite values.
Results may differ from the reference program's by a relative error of at most 0.0076.
Values may be sent and summed in bfloat16 or wider, within the bound.
No kernel may reach another device: no remote copies, remote signals or barrier semaphores. Data moves between devices by JAX's collectives and lax.ppermute only.
A program may use at most 256 MiB of HBM per device.

```python
import math
import jax
import jax.numpy as jnp
import numpy as np
from jax import lax

C = 4096
TAPS = 128
SHORT = 3
GROUPS = 256
WINDOWS = 8
LENGTH = 4096
TOKENS = 32768


def strengthened(entries, own_key, source, target, blocks, factor):
    def block_of(position):
        return (jnp.arange(entries.shape[position]) // (entries.shape[position] // blocks)).reshape((-1,) + (1,) * (entries.ndim - 1 - position))

    one_side = jax.random.permutation(own_key, blocks)[block_of(target)]
    other_side = (block_of(target) + blocks // 2) % blocks
    return jnp.where((block_of(source) == one_side) | (block_of(source) == other_side), factor * entries, entries)


def level_of(rng, dims, split, smallest, high):
    def one(dim, blocks):
        heights = jax.random.uniform(jax.random.fold_in(jax.random.fold_in(rng, 6), dim), (blocks,), jnp.float32, smallest / len(split), high / len(split))
        return jnp.repeat(jnp.exp(heights), dims[dim] // blocks).reshape((-1,) + (1,) * (len(dims) - dim - 1))

    gain = one(*split[0])
    for cut in split[1:]:
        gain = gain * one(*cut)
    return gain


def bell_draw(own_key, extent, spread, limit, shards=(), held_as=jnp.bfloat16):
    level = level_of(own_key, extent, shards, -0.22, 0.18) if shards else 1.0
    drawn = jax.random.normal(own_key, extent, jnp.float32) * spread * level
    return jnp.minimum(jnp.maximum(drawn, -limit), limit).astype(held_as)


def gaussian_with(stream_key, extent, deviation, limit, shards, heavy, held_as=jnp.bfloat16):
    values = deviation * jax.random.normal(stream_key, extent, jnp.float32)
    if shards:
        values = values * level_of(stream_key, extent, shards, -0.22, 0.18)
    return jnp.clip(strengthened(values, jax.random.fold_in(stream_key, 3), *heavy), -limit, limit).astype(held_as)


def setup_inputs(seed: int = 0) -> dict:
    seeds = jax.random.split(jax.random.key(seed), 5)
    return {
        "streams": bell_draw(seeds[0], (WINDOWS, LENGTH, 3 * C), 1.0, 6.0, ((0, 8), (1, 16))),
        "cotangent": gaussian_with(seeds[1], (WINDOWS, LENGTH, C), 1.0, 6.0, ((0, 8), (1, 16)), (1, 2, 16, 2.0)),
        "filters": bell_draw(seeds[2], (GROUPS, TAPS), 0.09, 0.54, ((0, 128),), jnp.float32),
        "short_taps": bell_draw(seeds[3], (SHORT, 3 * C), 0.6, 3.6, ((1, 128),), jnp.float32),
    }


def build_kernels(filters, tap_count):
    narrow = filters.astype(jnp.bfloat16)
    row_index = np.arange(tap_count)[:, None]
    col_index = np.arange(2 * tap_count)[None, :]
    kernels = []
    for lag_table in (row_index + tap_count - col_index, col_index - row_index):
        usable = (lag_table >= 0) & (lag_table < tap_count)
        picked = narrow[:, np.clip(lag_table, 0, tap_count - 1)]
        kernels.append(jnp.where(usable[None], picked, jnp.zeros((), jnp.bfloat16)))
    return (kernels[0], kernels[1])

def block_pairs(padded, tap_count):
    row_total = padded.shape[0] - tap_count
    block_count = row_total // tap_count
    leading = padded[:row_total].reshape(block_count, tap_count, padded.shape[1])
    trailing = padded[tap_count:].reshape(block_count, tap_count, padded.shape[1])
    return jnp.concatenate([leading, trailing], axis=1)

def apply_kernel(kernel, paired, group_count):
    block_count, span_rows, channels = paired.shape
    grouped = paired.reshape(block_count, span_rows, group_count, channels // group_count).astype(jnp.float32)
    mapped = jnp.einsum('gij,bjgc->bigc', kernel.astype(jnp.float32), grouped, precision=lax.Precision.HIGHEST)
    return mapped.reshape(block_count * kernel.shape[1], channels)

def diagonal_sums(moment, tap_count):
    row_index = np.arange(tap_count)[:, None]
    lag_index = np.arange(tap_count)[None, :]
    picked = moment[:, row_index, row_index + tap_count - lag_index]
    return lax.optimization_barrier(jnp.sum(picked, axis=1))

def window_pass(stream, grad_out, kernel_ahead, kernel_behind, short_taps, group_count, tap_count):
    length = stream.shape[0]
    channels = grad_out.shape[1]
    extended = jnp.concatenate([jnp.zeros((2, stream.shape[1]), jnp.bfloat16), stream], axis=0)
    feats = (short_taps[0] * extended[2:] + short_taps[1] * extended[1:-1] + short_taps[2] * extended[:-2]).astype(jnp.bfloat16)
    first = feats[:, :channels].astype(jnp.float32)
    second = feats[:, channels:2 * channels].astype(jnp.float32)
    values = feats[:, 2 * channels:].astype(jnp.float32)
    mixed = (first * values).astype(jnp.bfloat16)
    padded = jnp.concatenate([jnp.zeros((tap_count, channels), jnp.bfloat16), mixed], axis=0)
    paired = block_pairs(padded, tap_count)
    hidden = apply_kernel(kernel_ahead, paired, group_count)
    result = (second * hidden).astype(jnp.bfloat16)
    grad_f = grad_out.astype(jnp.float32)
    gated = (grad_f * second).astype(jnp.bfloat16)
    second_grad = grad_f * hidden
    gpadded = jnp.concatenate([gated, jnp.zeros((tap_count, channels), jnp.bfloat16)], axis=0)
    mixed_grad = apply_kernel(kernel_behind, block_pairs(gpadded, tap_count), group_count)
    feat_grad = jnp.concatenate([mixed_grad * values, second_grad, mixed_grad * first], axis=1)
    grad_ext = jnp.concatenate([feat_grad, jnp.zeros((2, feat_grad.shape[1]), jnp.float32)], axis=0)
    stream_grad = (short_taps[0] * feat_grad + short_taps[1] * grad_ext[1:length + 1] + short_taps[2] * grad_ext[2:length + 2]).astype(jnp.bfloat16)
    short_part = jnp.stack([lax.optimization_barrier(jnp.sum(feat_grad * extended[2 - offset:2 - offset + length].astype(jnp.float32), axis=0)) for offset in range(3)])
    block_count = length // tap_count
    gate_blocks = gated.reshape(block_count, tap_count, group_count, channels // group_count).astype(jnp.float32)
    mixed_blocks = paired.reshape(block_count, 2 * tap_count, group_count, channels // group_count).astype(jnp.float32)
    moment = jnp.einsum('bigc,bjgc->gij', gate_blocks, mixed_blocks, precision=lax.Precision.HIGHEST)
    filter_part = diagonal_sums(moment, tap_count)
    return (result, stream_grad, filter_part, short_part)

def reference(streams, cotangent, filters, short_taps):
    tap_count = filters.shape[1]
    group_count = filters.shape[0]
    kernel_ahead, kernel_behind = build_kernels(filters, tap_count)

    def per_window(operands):
        return window_pass(operands[0], operands[1], kernel_ahead, kernel_behind, short_taps, group_count, tap_count)
    result, stream_grad, filter_parts, short_parts = lax.map(per_window, (streams, cotangent))
    factor = 1.0 / math.sqrt(TOKENS)
    filter_grad = lax.optimization_barrier(jnp.sum(filter_parts, axis=0)) * factor
    short_grad = lax.optimization_barrier(jnp.sum(short_parts, axis=0)) * factor
    return (result, stream_grad, filter_grad, short_grad)
```

```python
import functools
import math

import jax
import jax.numpy as jnp
import numpy as np
from jax import lax
from jax.experimental import pallas as pl
from jax.experimental.pallas import tpu as pltpu
from jax.sharding import PartitionSpec as P

F32, BF16 = jnp.float32, jnp.bfloat16
LANES = 128
PACK = 16
BLOCK = 32


def shifted(value, axis, by):
    length = lax.axis_size(axis)
    pairs = [(i, i + by) for i in range(length) if 0 <= i + by < length]
    return lax.ppermute(value, axis, pairs)


def pick_groups(product, block, per_group):
    lane = lax.broadcasted_iota(jnp.int32, (block, LANES), 1)
    total = product[:block]
    for g in range(1, LANES // per_group):
        total = jnp.where(lane >= g * per_group, product[g * block : (g + 1) * block], total)
    return total


def featurized(x, at, count, tap):
    return (
        tap[0] * x[pl.ds(at, count)] + tap[1] * x[pl.ds(at - 1, count)] + tap[2] * x[pl.ds(at - 2, count)]
    ).astype(BF16)


def spans(ref, first, count, width):
    return jnp.concatenate([ref[(first + i) * BLOCK : (first + i) * BLOCK + width] for i in range(count)], axis=1)


def kernel(
    steps, width, rows, halo, taps, per_group,
    first_ref, second_ref, values_ref, cot_ref, before_ref, after_ref, ta_ref, tb_ref, tc_ref, filters_ref, turn_ref,
    result_ref, grad_ref, fgrad_ref, sgrad_ref,
    xa, xb, xc, fa, fb, fc, mixed, gated, ahead, behind, fga, fgb, fgc, masked, held, sems,
):
    step = pl.program_id(0)
    groups = LANES // per_group
    blocks = rows // BLOCK
    span = taps + BLOCK
    reach = taps + PACK
    channels = steps * width
    row = lax.broadcasted_iota(jnp.int32, (BLOCK, taps), 0)
    col = lax.broadcasted_iota(jnp.int32, (BLOCK, taps), 1)
    zero = jnp.zeros((BLOCK, taps), F32)
    lane_group = lax.broadcasted_iota(jnp.int32, (BLOCK, LANES), 1) // per_group

    def inner(part):
        lanes = slice(part * LANES, (part + 1) * LANES)
        tap_a, tap_b, tap_c = ([ref[s : s + 1, lanes] for s in range(3)] for ref in (ta_ref, tb_ref, tc_ref))

        xa[:halo] = before_ref[:halo, lanes].astype(F32)
        xa[halo : halo + rows] = first_ref[:, lanes].astype(F32)
        xa[halo + rows :] = after_ref[2 * halo : 2 * halo + PACK, lanes].astype(F32)
        xc[:halo] = before_ref[halo : 2 * halo, lanes].astype(F32)
        xc[halo : halo + rows] = values_ref[:, lanes].astype(F32)
        xc[halo + rows :] = after_ref[2 * halo + PACK : 2 * halo + 2 * PACK, lanes].astype(F32)
        xb[:PACK] = before_ref[2 * halo : 2 * halo + PACK, lanes].astype(F32)
        xb[PACK : PACK + rows] = second_ref[:, lanes].astype(F32)
        xb[PACK + rows :] = after_ref[:halo, lanes].astype(F32)

        for r in range(0, taps + rows + PACK, PACK):
            a = featurized(xa, halo - taps + r, PACK, tap_a)
            c = featurized(xc, halo - taps + r, PACK, tap_c)
            mixed[r : r + PACK] = (a.astype(F32) * c.astype(F32)).astype(BF16)
            if r >= taps:
                fa[r - taps : r - taps + PACK] = a
                fc[r - taps : r - taps + PACK] = c
        for r in range(0, rows + halo, PACK):
            b = featurized(xb, PACK + r, PACK, tap_b)
            if r < rows:
                cot = cot_ref[r : r + PACK, lanes]
                fb[r : r + PACK] = b
            else:
                cot = after_ref[halo + r - rows : halo + r - rows + PACK, lanes]
            gated[r : r + PACK] = (b.astype(F32) * cot.astype(F32)).astype(BF16)

        straight = filters_ref[part * groups : (part + 1) * groups]
        reverse = jnp.dot(straight.astype(BF16), turn_ref[...], preferred_element_type=F32)
        for g in range(groups):
            at = slice(g * BLOCK, (g + 1) * BLOCK)
            wheel = pltpu.roll(jnp.broadcast_to(reverse[g : g + 1], (BLOCK, taps)), 0, 1, stride=1, stride_axis=0)
            ahead[at, :taps] = jnp.where(col > row, wheel, zero).astype(BF16)
            ahead[at, taps:] = jnp.where(col > row, zero, wheel).astype(BF16)
            wheel = pltpu.roll(jnp.broadcast_to(straight[g : g + 1], (BLOCK, taps)), 0, 1, stride=1, stride_axis=0)
            behind[at, :taps] = jnp.where(col >= row, wheel, zero).astype(BF16)
            behind[at, taps:] = jnp.where(col >= row, zero, wheel).astype(BF16)

        toeplitz = ahead[:, :span]
        for b in range(0, blocks, 2):
            product = jnp.dot(toeplitz, spans(mixed, b, 2, span), preferred_element_type=F32)
            for i in range(2):
                at = slice((b + i) * BLOCK, (b + i + 1) * BLOCK)
                hidden = pick_groups(product[:, i * LANES : (i + 1) * LANES], BLOCK, per_group)
                result_ref[at, lanes] = (fb[at].astype(F32) * hidden).astype(BF16)
                fgb[at] = cot_ref[at, lanes].astype(F32) * hidden
        heads = jnp.concatenate([ahead[g * BLOCK : g * BLOCK + PACK, :reach] for g in range(groups)], axis=0)
        product = jnp.dot(heads, mixed[rows : rows + reach], preferred_element_type=F32)
        fgb[rows:] = after_ref[halo : halo + PACK, lanes].astype(F32) * pick_groups(product, PACK, per_group)

        toeplitz = behind[:, :span]
        for b in range(0, blocks, 2):
            product = jnp.dot(toeplitz, spans(gated, b, 2, span), preferred_element_type=F32)
            for i in range(2):
                at = slice((b + i) * BLOCK, (b + i + 1) * BLOCK)
                grad = pick_groups(product[:, i * LANES : (i + 1) * LANES], BLOCK, per_group)
                fga[at] = grad * fc[at].astype(F32)
                fgc[at] = grad * fa[at].astype(F32)
        heads = jnp.concatenate([behind[g * BLOCK : g * BLOCK + PACK, :reach] for g in range(groups)], axis=0)
        product = jnp.dot(heads, gated[rows : rows + reach], preferred_element_type=F32)
        grad = pick_groups(product, PACK, per_group)
        fga[rows:] = grad * fc[rows:].astype(F32)
        fgc[rows:] = grad * fa[rows:].astype(F32)

        for b in range(blocks):
            block = gated[b * BLOCK : (b + 1) * BLOCK].astype(F32)
            for g in range(groups):
                masked[g * BLOCK : (g + 1) * BLOCK, b * LANES : (b + 1) * LANES] = jnp.where(
                    lane_group == g, block, 0.0
                ).astype(BF16)
        moment = lax.dot_general(
            masked[...], spans(mixed, 0, blocks, span), (((1,), (1,)), ((), ())), preferred_element_type=F32
        )
        for g in range(groups):
            at = slice(g * BLOCK, (g + 1) * BLOCK)
            later = jnp.concatenate([moment[at, taps:], jnp.zeros((BLOCK, taps - BLOCK), F32)], axis=1)
            wheel = jnp.where(col > row, moment[at, :taps], later)
            turned = wheel[:8]
            for p in range(8, BLOCK, 8):
                turned = turned + pltpu.roll(wheel[p : p + 8], taps - p, 1)
            for p in (4, 2, 1):
                turned = turned + pltpu.roll(pltpu.roll(turned, taps - p, 1), 8 - p, 0)
            fgrad_ref[part * groups + g : part * groups + g + 1] = turned[:1]

        column = pl.multiple_of(step * width + part * LANES, LANES)
        for which, (fg, x, start, tap) in enumerate(
            ((fga, xa, halo, tap_a), (fgb, xb, PACK, tap_b), (fgc, xc, halo, tap_c))
        ):
            sums = [jnp.zeros((8, LANES), F32) for _ in range(3)]
            for r in range(0, rows, PACK):
                near = [fg[pl.ds(r + s, PACK)] for s in range(3)]
                grad = tap[0] * near[0] + tap[1] * near[1] + tap[2] * near[2]
                held[r : r + PACK, pl.ds(which * channels + column, LANES)] = grad.astype(BF16)
                own = x[start + r : start + r + PACK]
                for s in range(3):
                    term = near[s] * own
                    sums[s] = sums[s] + (term[:8] + term[8:])
            for s in range(3):
                sgrad_ref[which, s : s + 1, lanes] = jnp.sum(sums[s], axis=0, keepdims=True)

    for part in range(width // LANES):
        inner(part)

    def copy(at, which):
        columns = pl.ds(pl.multiple_of(which * channels + at * width, LANES), width)
        return pltpu.make_async_copy(held.at[:, columns], grad_ref.at[:, columns], sems.at[which])

    for which in range(3):
        copy(step, which).start()

    @pl.when(step == steps - 1)
    def _():
        for which in range(3):
            columns = pl.ds(which * channels, channels)
            pltpu.make_async_copy(held.at[:, columns], grad_ref.at[:, columns], sems.at[which]).wait()


def local(stream, cot, before, after, filters, tap_rows, halo, width=2 * LANES):
    rows, channels = cot.shape
    group_count, taps = filters.shape
    per_group = channels // group_count
    steps = channels // width
    groups = width // per_group
    span = taps + BLOCK
    index = np.arange(taps)
    turn = jnp.asarray(index[:, None] == (-index[None, :]) % taps, BF16)

    def column(offset, height):
        return pl.BlockSpec((height, width), lambda j: (0, offset * steps + j))

    return pl.pallas_call(
        functools.partial(kernel, steps, width, rows, halo, taps, per_group),
        grid=(steps,),
        in_specs=[column(w, rows) for w in range(3)]
        + [column(0, rows), column(0, before.shape[0]), column(0, after.shape[0])]
        + [column(w, 3) for w in range(3)]
        + [pl.BlockSpec((groups, taps), lambda j: (j, 0)), pl.BlockSpec((taps, taps), lambda j: (0, 0))],
        out_specs=[
            column(0, rows),
            pl.BlockSpec(memory_space=pl.ANY),
            pl.BlockSpec((groups, taps), lambda j: (j, 0)),
            pl.BlockSpec((3, 3, width), lambda j: (0, 0, j)),
        ],
        out_shape=[
            jax.ShapeDtypeStruct((rows, channels), BF16),
            jax.ShapeDtypeStruct((rows, 3 * channels), BF16),
            jax.ShapeDtypeStruct((group_count, taps), F32),
            jax.ShapeDtypeStruct((3, 3, channels), F32),
        ],
        scratch_shapes=[
            pltpu.VMEM((halo + rows + PACK, LANES), F32),
            pltpu.VMEM((PACK + rows + halo, LANES), F32),
            pltpu.VMEM((halo + rows + PACK, LANES), F32),
            pltpu.VMEM((rows + PACK, LANES), BF16),
            pltpu.VMEM((rows, LANES), BF16),
            pltpu.VMEM((rows + PACK, LANES), BF16),
            pltpu.VMEM((taps + rows + PACK, LANES), BF16),
            pltpu.VMEM((rows + halo, LANES), BF16),
            pltpu.VMEM((LANES // per_group * BLOCK, 2 * taps), BF16),
            pltpu.VMEM((LANES // per_group * BLOCK, 2 * taps), BF16),
            pltpu.VMEM((rows + PACK, LANES), F32),
            pltpu.VMEM((rows + PACK, LANES), F32),
            pltpu.VMEM((rows + PACK, LANES), F32),
            pltpu.VMEM((LANES // per_group * BLOCK, rows // BLOCK * LANES), BF16),
            pltpu.VMEM((rows, 3 * channels), BF16),
            pltpu.SemaphoreType.DMA((3,)),
        ],
        compiler_params=pltpu.CompilerParams(vmem_limit_bytes=48 * 1024 * 1024),
        name="hyena_block",
    )(stream, stream, stream, cot, before, after, tap_rows, tap_rows, tap_rows, filters, turn)


def on_device(streams, cotangent, filters, short_taps):
    stream, cot = streams[0], cotangent[0]
    rows, channels = cot.shape
    own_groups, taps = filters.shape
    own_taps = short_taps.shape[1]
    device_count = lax.axis_size("fsdp") * lax.axis_size("ctx")
    group_count = own_groups * device_count
    halo = taps + PACK
    first, second, values = (stream[:, w * channels : (w + 1) * channels] for w in range(3))

    before = shifted(
        jnp.concatenate([first[rows - halo :], values[rows - halo :], second[rows - PACK :]], axis=0), "ctx", 1
    )
    after = shifted(jnp.concatenate([second[:halo], cot[:halo], first[:PACK], values[:PACK]], axis=0), "ctx", -1)

    padding = -own_taps % LANES
    own = jnp.concatenate(
        [filters.reshape(1, -1), jnp.pad(short_taps, ((0, 0), (0, padding))).reshape(1, -1)], axis=1
    )
    whole = lax.all_to_all(
        jnp.broadcast_to(own, (device_count, own.shape[1])), ("fsdp", "ctx"), 0, 0, tiled=True
    )
    whole_filters = whole[:, : own_groups * taps].reshape(group_count, taps)
    whole_taps = whole[:, own_groups * taps :].reshape(device_count, 3, own_taps + padding)[:, :, :own_taps]
    whole_taps = whole_taps.transpose(1, 0, 2).reshape(3, device_count * own_taps)

    result, stream_grad, filter_part, short_part = local(stream, cot, before, after, whole_filters, whole_taps, halo)

    filter_part = filter_part.reshape(device_count, own_groups * taps)
    short_part = short_part.transpose(1, 0, 2).reshape(3, device_count, own_taps).transpose(1, 0, 2)
    short_part = jnp.pad(short_part, ((0, 0), (0, 0), (0, padding))).reshape(device_count, -1)
    terms = lax.all_to_all(
        jnp.concatenate([filter_part, short_part], axis=1), ("fsdp", "ctx"), 0, 0, tiled=True
    )
    factor = 1.0 / math.sqrt(device_count * rows)
    total = jnp.sum(terms, axis=0) * factor
    filter_grad = jnp.roll(total[: own_groups * taps].reshape(own_groups, taps)[:, ::-1], 1, axis=1)
    short_grad = total[own_groups * taps :].reshape(3, own_taps + padding)[:, :own_taps]
    return (result[None], stream_grad[None], filter_grad, short_grad)


def solution(mesh):
    in_specs = (
        P("fsdp", "ctx", None),
        P("fsdp", "ctx", None),
        P(("fsdp", "ctx"), None),
        P(None, ("fsdp", "ctx")),
    )
    out_specs = (
        P("fsdp", "ctx", None),
        P("fsdp", "ctx", None),
        P(("fsdp", "ctx"), None),
        P(None, ("fsdp", "ctx")),
    )
    return jax.shard_map(
        on_device, mesh=mesh, in_specs=in_specs, out_specs=out_specs, check_vma=False
    )
```

```python
import functools
import math

import jax
import jax.numpy as jnp
import numpy as np
from jax import lax
from jax.experimental import pallas as pl
from jax.experimental.pallas import tpu as pltpu
from jax.sharding import PartitionSpec as P

F32, BF16 = jnp.float32, jnp.bfloat16
LANES = 128
PACK = 16
BLOCK = 32
PITCH = BLOCK + 8
LEAD = 8
PARTS = 1
VMEM = 56 * 1024 * 1024


def shifted(value, axis, by):
    length = lax.axis_size(axis)
    pairs = [(i, i + by) for i in range(length) if 0 <= i + by < length]
    return lax.ppermute(value, axis, pairs)


def pick_groups(product, block, per_group):
    lane = lax.broadcasted_iota(jnp.int32, (block, LANES), 1)
    total = product[:block]
    for g in range(1, LANES // per_group):
        total = jnp.where(lane >= g * per_group, product[g * block : (g + 1) * block], total)
    return total


def featurized(x, at, count, tap):
    return (
        tap[0] * x[pl.ds(at, count)] + tap[1] * x[pl.ds(at - 1, count)] + tap[2] * x[pl.ds(at - 2, count)]
    ).astype(BF16)


def spans(ref, first, count, width):
    return jnp.concatenate([ref[(first + i) * BLOCK : (first + i) * BLOCK + width] for i in range(count)], axis=1)


def taps_of(refs, lanes):
    return [[ref[s : s + 1, lanes] for s in range(3)] for ref in refs]


def toeplitz_kernel(taps, filters_ref, turn_ref, ahead_ref, behind_ref):
    row = lax.broadcasted_iota(jnp.int32, (BLOCK, taps), 0)
    col = lax.broadcasted_iota(jnp.int32, (BLOCK, taps), 1)
    zero = jnp.zeros((BLOCK, taps), F32)
    straight = filters_ref[...]
    reverse = jnp.dot(straight.astype(BF16), turn_ref[...], preferred_element_type=F32)
    for g in range(straight.shape[0]):
        at = slice(g * BLOCK, (g + 1) * BLOCK)
        wheel = pltpu.roll(jnp.broadcast_to(reverse[g : g + 1], (BLOCK, taps)), 0, 1, stride=1, stride_axis=0)
        ahead_ref[at, :taps] = jnp.where(col > row, wheel, zero).astype(BF16)
        ahead_ref[at, taps:] = jnp.where(col > row, zero, wheel).astype(BF16)
        wheel = pltpu.roll(jnp.broadcast_to(straight[g : g + 1], (BLOCK, taps)), 0, 1, stride=1, stride_axis=0)
        behind_ref[at, :taps] = jnp.where(col >= row, wheel, zero).astype(BF16)
        behind_ref[at, taps:] = jnp.where(col >= row, zero, wheel).astype(BF16)


def toeplitz_blocks(filters, batch=64):
    group_count, taps = filters.shape
    index = np.arange(taps)
    turn = jnp.asarray(index[:, None] == (-index[None, :]) % taps, BF16)
    out = pl.BlockSpec((batch * BLOCK, 2 * taps), lambda j: (j, 0))
    shape = jax.ShapeDtypeStruct((group_count * BLOCK, 2 * taps), BF16)
    return pl.pallas_call(
        functools.partial(toeplitz_kernel, taps),
        grid=(group_count // batch,),
        in_specs=[pl.BlockSpec((batch, taps), lambda j: (j, 0)), pl.BlockSpec((taps, taps), lambda j: (0, 0))],
        out_specs=[out, out],
        out_shape=[shape, shape],
        compiler_params=pltpu.CompilerParams(vmem_limit_bytes=VMEM),
        cost_estimate=pl.CostEstimate(flops=10**9, bytes_accessed=10**7, transcendentals=0),
        name="toeplitz_blocks",
    )(filters, turn)


def edge_kernel(
    width, taps,
    first_lead, first_tail, values_lead, values_tail, first_head, values_head, second_head, second_next,
    cot_head, cot_next, tail_a, tail_b, tail_c, ta_ref, tb_ref, tc_ref,
    mixed_ref, gated_ref,
    xa, xb, xc, xs, xt, tile,
):
    for part in range(width // LANES):
        lanes = slice(part * LANES, (part + 1) * LANES)
        tap_a, tap_b, tap_c = taps_of((ta_ref, tb_ref, tc_ref), lanes)
        for x, lead, tail in ((xa, first_lead, first_tail), (xc, values_lead, values_tail)):
            x[:PACK] = lead[:, lanes].astype(F32)
            x[PACK:] = tail[:, lanes].astype(F32)
        for r in range(0, taps, PACK):
            a = featurized(xa, PACK + r, PACK, tap_a)
            c = featurized(xc, PACK + r, PACK, tap_c)
            mixed_ref[r : r + PACK, lanes] = (a.astype(F32) * c.astype(F32)).astype(BF16)
        xb[:LEAD] = tail_b[:, lanes]
        xb[LEAD : LEAD + taps] = second_head[:, lanes].astype(F32)
        xb[LEAD + taps :] = second_next[:, lanes].astype(F32)
        for r in range(0, taps, PACK):
            b = featurized(xb, LEAD + r, PACK, tap_b)
            gated_ref[r : r + PACK, lanes] = (b.astype(F32) * cot_head[r : r + PACK, lanes].astype(F32)).astype(BF16)
        b = featurized(xb, LEAD + taps, PACK, tap_b)
        for x, lead, head in ((xs, tail_a, first_head), (xt, tail_c, values_head)):
            x[:LEAD] = lead[:, lanes]
            x[LEAD:] = head[:, lanes].astype(F32)
        tile[...] = jnp.zeros_like(tile)
        tile[:1] = (b.astype(F32) * cot_next[:, lanes].astype(F32))[:1]
        tile[1:3] = featurized(xs, LEAD, PACK, tap_a).astype(F32)[:2]
        tile[3:5] = featurized(xt, LEAD, PACK, tap_c).astype(F32)[:2]
        tile[5:7] = cot_head[:PACK, lanes].astype(F32)[:2]
        gated_ref[taps:, lanes] = tile[...].astype(BF16)


def edges(part, stream, cot, tails, tap_rows, taps, width=8 * LANES):
    rows, channels = cot.shape
    all_steps = channels // width
    steps = all_steps // PARTS

    def column(which, height, at=0):
        return pl.BlockSpec((height, width), lambda j: (at, which * all_steps + part * steps + j))

    lead, last = (rows - taps) // PACK - 1, rows // taps - 1
    own = lambda j: (0, j)
    return pl.pallas_call(
        functools.partial(edge_kernel, width, taps),
        grid=(steps,),
        in_specs=[column(0, PACK, lead), column(0, taps, last), column(2, PACK, lead), column(2, taps, last)]
        + [column(0, PACK), column(2, PACK), column(1, taps), column(1, PACK, taps // PACK)]
        + [column(0, taps), column(0, PACK, taps // PACK)]
        + [column(w, LEAD) for w in range(3)]
        + [column(w, 3) for w in range(3)],
        out_specs=[pl.BlockSpec((taps, width), own), pl.BlockSpec((taps + PACK, width), own)],
        out_shape=[
            jax.ShapeDtypeStruct((taps, steps * width), BF16),
            jax.ShapeDtypeStruct((taps + PACK, steps * width), BF16),
        ],
        scratch_shapes=[
            pltpu.VMEM((PACK + taps, LANES), F32),
            pltpu.VMEM((LEAD + taps + PACK, LANES), F32),
            pltpu.VMEM((PACK + taps, LANES), F32),
            pltpu.VMEM((LEAD + PACK, LANES), F32),
            pltpu.VMEM((LEAD + PACK, LANES), F32),
            pltpu.VMEM((PACK, LANES), F32),
        ],
        compiler_params=pltpu.CompilerParams(vmem_limit_bytes=VMEM),
        cost_estimate=pl.CostEstimate(flops=10**7, bytes_accessed=4 * 10**6, transcendentals=0),
        name="edges",
    )(*[stream] * 8, cot, cot, *[tails] * 3, *[tap_rows] * 3)


def main_kernel(
    part, steps, width, rows, channels, taps, per_group, aliased, *refs
):
    (first_ref, second_ref, values_ref, cot_ref, before_ref, after_ref, tail_a, tail_b, tail_c,
     ta_ref, tb_ref, tc_ref, ahead, behind) = refs[:14]
    result_ref, grad_ref, fgrad_ref, sgrad_ref = refs[14 + aliased : 18 + aliased]
    *buffers, wheels, held, sems = refs[18 + aliased :]
    step = pl.program_id(0)
    groups = LANES // per_group
    blocks = rows // BLOCK
    span = taps + BLOCK
    reach = taps + PACK
    inner_parts = width // LANES
    row = lax.broadcasted_iota(jnp.int32, (BLOCK, taps), 0)
    col = lax.broadcasted_iota(jnp.int32, (BLOCK, taps), 1)
    lane = lax.broadcasted_iota(jnp.int32, (BLOCK, LANES), 1)

    def diagonal_sums(at):
        for p in range(inner_parts):
            total = jnp.zeros((groups, taps), F32)
            for i in range(BLOCK):
                turned = wheels[pl.ds(p * groups * PITCH + i, groups, stride=PITCH), :]
                total = total + (pltpu.roll(turned, taps - i, 1) if i else turned)
            fgrad_ref[pl.ds(pl.multiple_of((at * inner_parts + p) * groups, groups), groups), :] = total

    diagonal_sums(jnp.maximum(step - 1, 0))

    def inner(p):
        lanes = slice(p * LANES, (p + 1) * LANES)
        xa, xb, xc, fa, fb, fc, mixed, gated, fga, fgb, fgc, masked, tile = (ref.at[p] for ref in buffers)
        tap_a, tap_b, tap_c = taps_of((ta_ref, tb_ref, tc_ref), lanes)
        for x, lead, own in ((xa, tail_a, first_ref), (xb, tail_b, second_ref), (xc, tail_c, values_ref)):
            x[:LEAD] = lead[:, lanes]
            x[LEAD:] = own[:, lanes].astype(F32)
        tile[:PACK] = after_ref[taps:, lanes].astype(F32)
        tile[PACK:] = jnp.zeros((PACK, LANES), F32)

        mixed[:taps] = before_ref[:, lanes]
        for r in range(0, rows, PACK):
            a = featurized(xa, LEAD + r, PACK, tap_a)
            c = featurized(xc, LEAD + r, PACK, tap_c)
            mixed[taps + r : taps + r + PACK] = (a.astype(F32) * c.astype(F32)).astype(BF16)
            fa[r : r + PACK] = a
            fc[r : r + PACK] = c
        mixed[taps + rows :] = (tile[1 : 1 + PACK] * tile[3 : 3 + PACK]).astype(BF16)
        for r in range(0, rows, PACK):
            b = featurized(xb, LEAD + r, PACK, tap_b)
            fb[r : r + PACK] = b
            gated[r : r + PACK] = (b.astype(F32) * cot_ref[r : r + PACK, lanes].astype(F32)).astype(BF16)
        gated[rows : rows + taps] = after_ref[:taps, lanes]
        gated[rows + taps :] = jnp.where(row[:PACK] == 0, tile[:PACK], 0.0).astype(BF16)

        top = p * groups * BLOCK

        toeplitz = ahead[top : top + groups * BLOCK, :span]
        for b in range(0, blocks, 2):
            product = jnp.dot(toeplitz, spans(mixed, b, 2, span), preferred_element_type=F32)
            for i in range(2):
                at = slice((b + i) * BLOCK, (b + i + 1) * BLOCK)
                hidden = pick_groups(product[:, i * LANES : (i + 1) * LANES], BLOCK, per_group)
                result_ref[at, lanes] = (fb[at].astype(F32) * hidden).astype(BF16)
                fgb[at] = cot_ref[at, lanes].astype(F32) * hidden
        heads = [slice(top + g * BLOCK, top + g * BLOCK + PACK) for g in range(groups)]
        product = jnp.dot(
            jnp.concatenate([ahead[at, :reach] for at in heads], axis=0),
            mixed[rows : rows + reach],
            preferred_element_type=F32,
        )
        fgb[rows:] = tile[5 : 5 + PACK] * pick_groups(product, PACK, per_group)

        toeplitz = behind[top : top + groups * BLOCK, :span]
        for b in range(0, blocks, 2):
            product = jnp.dot(toeplitz, spans(gated, b, 2, span), preferred_element_type=F32)
            for i in range(2):
                at = slice((b + i) * BLOCK, (b + i + 1) * BLOCK)
                grad = pick_groups(product[:, i * LANES : (i + 1) * LANES], BLOCK, per_group)
                fga[at] = grad * fc[at].astype(F32)
                fgc[at] = grad * fa[at].astype(F32)
        product = jnp.dot(
            jnp.concatenate([behind[at, :reach] for at in heads], axis=0),
            gated[rows : rows + reach],
            preferred_element_type=F32,
        )
        grad = pick_groups(product, PACK, per_group)
        fga[rows:] = grad * tile[3 : 3 + PACK]
        fgc[rows:] = grad * tile[1 : 1 + PACK]

        for b in range(blocks):
            block = gated[b * BLOCK : (b + 1) * BLOCK].astype(F32)
            for g in range(groups):
                here = (lane >= g * per_group) & (lane < (g + 1) * per_group)
                masked[g * BLOCK : (g + 1) * BLOCK, b * LANES : (b + 1) * LANES] = jnp.where(here, block, 0.0).astype(
                    BF16
                )
        moment = lax.dot_general(
            masked[...], spans(mixed, 0, blocks, span), (((1,), (1,)), ((), ())), preferred_element_type=F32
        )
        for g in range(groups):
            at = slice(g * BLOCK, (g + 1) * BLOCK)
            later = jnp.concatenate([moment[at, taps:], jnp.zeros((BLOCK, taps - BLOCK), F32)], axis=1)
            start = (p * groups + g) * PITCH
            wheels[start : start + BLOCK] = jnp.where(col > row, moment[at, :taps], later)

        column = pl.multiple_of(step * width + p * LANES, LANES)
        for which, (fg, x, tap) in enumerate(((fga, xa, tap_a), (fgb, xb, tap_b), (fgc, xc, tap_c))):
            sums = [jnp.zeros((8, LANES), F32) for _ in range(3)]
            for r in range(0, rows, PACK):
                near = [fg[pl.ds(r + s, PACK)] for s in range(3)]
                grad = tap[0] * near[0] + tap[1] * near[1] + tap[2] * near[2]
                held[r : r + PACK, pl.ds(which * steps * width + column, LANES)] = grad.astype(BF16)
                own = x[LEAD + r : LEAD + r + PACK]
                for s in range(3):
                    term = near[s] * own
                    sums[s] = sums[s] + (term[:8] + term[8:])
            for s in range(3):
                sgrad_ref[which, s : s + 1, lanes] = jnp.sum(sums[s], axis=0, keepdims=True)

    for p in range(inner_parts):
        inner(p)

    def copy(which, first, count):
        source = pl.ds(pl.multiple_of(which * steps * width + first, LANES), count)
        target = pl.ds(pl.multiple_of(which * channels + part * steps * width + first, LANES), count)
        return pltpu.make_async_copy(held.at[:, source], grad_ref.at[:, target], sems.at[which])

    for which in range(3):
        copy(which, step * width, width).start()

    @pl.when(step == steps - 1)
    def _():
        diagonal_sums(step)
        for which in range(3):
            copy(which, 0, steps * width).wait()


def main(part, stream, cot, before, after, tails, tap_rows, ahead, behind, earlier, taps, per_group, width=2 * LANES):
    rows, channels = cot.shape
    all_steps = channels // width
    steps = all_steps // PARTS
    groups = width // per_group
    offset = part * steps

    def column(which, height):
        return pl.BlockSpec((height, width), lambda j: (0, which * all_steps + offset + j))

    def own(height):
        return pl.BlockSpec((height, width), lambda j: (0, j))

    table = pl.BlockSpec((groups * BLOCK, 2 * taps), lambda j: (offset + j, 0))
    stacked = LANES // per_group * BLOCK
    inner = width // LANES
    outs = [jax.ShapeDtypeStruct((rows, channels), BF16), jax.ShapeDtypeStruct((rows, 3 * channels), BF16)]
    return pl.pallas_call(
        functools.partial(main_kernel, part, steps, width, rows, channels, taps, per_group, len(earlier)),
        grid=(steps,),
        in_specs=[column(w, rows) for w in range(3)]
        + [column(0, rows), own(taps), own(taps + PACK)]
        + [column(w, LEAD) for w in range(3)]
        + [column(w, 3) for w in range(3)]
        + [table, table]
        + [pl.BlockSpec(memory_space=pl.ANY)] * len(earlier),
        out_specs=[
            column(0, rows),
            pl.BlockSpec(memory_space=pl.ANY),
            pl.BlockSpec((steps * groups, taps), lambda j: (0, 0)),
            pl.BlockSpec((3, 3, width), lambda j: (0, 0, j)),
        ],
        out_shape=outs
        + [
            jax.ShapeDtypeStruct((steps * groups, taps), F32),
            jax.ShapeDtypeStruct((3, 3, steps * width), F32),
        ],
        scratch_shapes=[pltpu.VMEM((inner, LEAD + rows, LANES), F32)] * 3
        + [pltpu.VMEM((inner, rows, LANES), BF16)] * 3
        + [pltpu.VMEM((inner, taps + rows + PACK, LANES), BF16)] * 2
        + [pltpu.VMEM((inner, rows + PACK, LANES), F32)] * 3
        + [
            pltpu.VMEM((inner, stacked, rows // BLOCK * LANES), BF16),
            pltpu.VMEM((inner, 2 * PACK, LANES), F32),
            pltpu.VMEM((width // per_group * PITCH, taps), F32),
            pltpu.VMEM((rows, 3 * steps * width), BF16),
            pltpu.SemaphoreType.DMA((3,)),
        ],
        input_output_aliases={14 + i: i for i in range(len(earlier))},
        compiler_params=pltpu.CompilerParams(vmem_limit_bytes=VMEM),
        cost_estimate=pl.CostEstimate(flops=10**10, bytes_accessed=2 * 10**7, transcendentals=0),
        name="hyena_main",
    )(*[stream] * 3, cot, before, after, *[tails] * 3, *[tap_rows] * 3, ahead, behind, *earlier)


def on_device(streams, cotangent, filters, short_taps):
    stream, cot = streams[0], cotangent[0]
    rows, channels = cot.shape
    own_groups, taps = filters.shape
    own_taps = short_taps.shape[1]
    device_count = lax.axis_size("fsdp") * lax.axis_size("ctx")
    group_count = own_groups * device_count
    per_group = channels // group_count

    tails = shifted(stream[rows - 2 :], "ctx", 1)
    tails = jnp.pad(tails.astype(F32), ((LEAD - 2, 0), (0, 0)))

    padding = -own_taps % LANES
    own = jnp.concatenate(
        [filters.reshape(1, -1), jnp.pad(short_taps, ((0, 0), (0, padding))).reshape(1, -1)], axis=1
    )
    whole = lax.all_to_all(
        jnp.broadcast_to(own, (device_count, own.shape[1])), ("fsdp", "ctx"), 0, 0, tiled=True
    )
    whole_filters = whole[:, : own_groups * taps].reshape(group_count, taps)
    whole_taps = whole[:, own_groups * taps :].reshape(device_count, 3, own_taps + padding)[:, :, :own_taps]
    whole_taps = whole_taps.transpose(1, 0, 2).reshape(3, device_count * own_taps)

    halos = []
    for part in range(PARTS):
        mixed_tail, gated_head = edges(part, stream, cot, tails, whole_taps, taps)
        halos.append((shifted(mixed_tail, "ctx", 1), shifted(gated_head, "ctx", -1)))
    ahead, behind = toeplitz_blocks(whole_filters)
    earlier, filter_parts, short_parts = (), [], []
    for part in range(PARTS):
        result, stream_grad, filter_part, short_part = main(
            part, stream, cot, *halos[part], tails, whole_taps, ahead, behind, earlier, taps, per_group
        )
        earlier = (result, stream_grad)
        filter_parts.append(filter_part)
        short_parts.append(short_part)

    filter_part = jnp.concatenate(filter_parts, axis=0).reshape(device_count, own_groups * taps)
    short_part = jnp.concatenate(short_parts, axis=2)
    short_part = short_part.transpose(1, 0, 2).reshape(3, device_count, own_taps).transpose(1, 0, 2)
    short_part = jnp.pad(short_part, ((0, 0), (0, 0), (0, padding))).reshape(device_count, -1)
    terms = lax.all_to_all(
        jnp.concatenate([filter_part, short_part], axis=1), ("fsdp", "ctx"), 0, 0, tiled=True
    )
    factor = 1.0 / math.sqrt(device_count * rows)
    total = jnp.sum(terms, axis=0) * factor
    filter_grad = jnp.roll(total[: own_groups * taps].reshape(own_groups, taps)[:, ::-1], 1, axis=1)
    short_grad = total[own_groups * taps :].reshape(3, own_taps + padding)[:, :own_taps]
    return (result[None], stream_grad[None], filter_grad, short_grad)


def solution(mesh):
    in_specs = (
        P("fsdp", "ctx", None),
        P("fsdp", "ctx", None),
        P(("fsdp", "ctx"), None),
        P(None, ("fsdp", "ctx")),
    )
    out_specs = (
        P("fsdp", "ctx", None),
        P("fsdp", "ctx", None),
        P(("fsdp", "ctx"), None),
        P(None, ("fsdp", "ctx")),
    )
    return jax.shard_map(
        on_device, mesh=mesh, in_specs=in_specs, out_specs=out_specs, check_vma=False
    )
```

```python
import functools
import math

import jax
import jax.numpy as jnp
import numpy as np
from jax import lax
from jax.experimental import pallas as pl
from jax.experimental.pallas import tpu as pltpu
from jax.sharding import PartitionSpec as P

F32, BF16 = jnp.float32, jnp.bfloat16
LANES = 128
PACK = 16
BLOCK = 32
PITCH = BLOCK + 8
LEAD = 8
PARTS = 1
VMEM = 24 * 1024 * 1024
MAIN_VMEM = 24 * 1024 * 1024


def shifted(value, axis, by):
    length = lax.axis_size(axis)
    pairs = [(i, i + by) for i in range(length) if 0 <= i + by < length]
    return lax.ppermute(value, axis, pairs)


def pick_groups(product, block, per_group):
    lane = lax.broadcasted_iota(jnp.int32, (block, LANES), 1)
    total = product[:block]
    for g in range(1, LANES // per_group):
        total = jnp.where(lane >= g * per_group, product[g * block : (g + 1) * block], total)
    return total


def featurized(x, at, count, tap):
    return (
        tap[0] * x[pl.ds(at, count)] + tap[1] * x[pl.ds(at - 1, count)] + tap[2] * x[pl.ds(at - 2, count)]
    ).astype(BF16)


def spans(ref, first, count, width):
    return jnp.concatenate([ref[(first + i) * BLOCK : (first + i) * BLOCK + width] for i in range(count)], axis=1)


def taps_of(refs, lanes):
    return [[ref[s : s + 1, lanes] for s in range(3)] for ref in refs]


def toeplitz_kernel(taps, filters_ref, turn_ref, ahead_ref, behind_ref):
    row = lax.broadcasted_iota(jnp.int32, (BLOCK, taps), 0)
    col = lax.broadcasted_iota(jnp.int32, (BLOCK, taps), 1)
    zero = jnp.zeros((BLOCK, taps), F32)
    straight = filters_ref[...]
    reverse = jnp.dot(straight.astype(BF16), turn_ref[...], preferred_element_type=F32)
    for g in range(straight.shape[0]):
        at = slice(g * BLOCK, (g + 1) * BLOCK)
        wheel = pltpu.roll(jnp.broadcast_to(reverse[g : g + 1], (BLOCK, taps)), 0, 1, stride=1, stride_axis=0)
        ahead_ref[at, :taps] = jnp.where(col > row, wheel, zero).astype(BF16)
        ahead_ref[at, taps:] = jnp.where(col > row, zero, wheel).astype(BF16)
        wheel = pltpu.roll(jnp.broadcast_to(straight[g : g + 1], (BLOCK, taps)), 0, 1, stride=1, stride_axis=0)
        behind_ref[at, :taps] = jnp.where(col >= row, wheel, zero).astype(BF16)
        behind_ref[at, taps:] = jnp.where(col >= row, zero, wheel).astype(BF16)


def toeplitz_blocks(filters, batch=64):
    group_count, taps = filters.shape
    index = np.arange(taps)
    turn = jnp.asarray(index[:, None] == (-index[None, :]) % taps, BF16)
    out = pl.BlockSpec((batch * BLOCK, 2 * taps), lambda j: (j, 0))
    shape = jax.ShapeDtypeStruct((group_count * BLOCK, 2 * taps), BF16)
    return pl.pallas_call(
        functools.partial(toeplitz_kernel, taps),
        grid=(group_count // batch,),
        in_specs=[pl.BlockSpec((batch, taps), lambda j: (j, 0)), pl.BlockSpec((taps, taps), lambda j: (0, 0))],
        out_specs=[out, out],
        out_shape=[shape, shape],
        compiler_params=pltpu.CompilerParams(vmem_limit_bytes=VMEM),
        cost_estimate=pl.CostEstimate(flops=10**9, bytes_accessed=10**7, transcendentals=0),
        name="toeplitz_blocks",
    )(filters, turn)


def edge_kernel(
    width, taps,
    first_lead, first_tail, values_lead, values_tail, first_head, values_head, second_head, second_next,
    cot_head, cot_next, tail_a, tail_b, tail_c, ta_ref, tb_ref, tc_ref,
    mixed_ref, gated_ref,
    xa, xb, xc, xs, xt, tile,
):
    for part in range(width // LANES):
        lanes = slice(part * LANES, (part + 1) * LANES)
        tap_a, tap_b, tap_c = taps_of((ta_ref, tb_ref, tc_ref), lanes)
        for x, lead, tail in ((xa, first_lead, first_tail), (xc, values_lead, values_tail)):
            x[:PACK] = lead[:, lanes].astype(F32)
            x[PACK:] = tail[:, lanes].astype(F32)
        for r in range(0, taps, PACK):
            a = featurized(xa, PACK + r, PACK, tap_a)
            c = featurized(xc, PACK + r, PACK, tap_c)
            mixed_ref[r : r + PACK, lanes] = (a.astype(F32) * c.astype(F32)).astype(BF16)
        xb[:LEAD] = tail_b[:, lanes]
        xb[LEAD : LEAD + taps] = second_head[:, lanes].astype(F32)
        xb[LEAD + taps :] = second_next[:, lanes].astype(F32)
        for r in range(0, taps, PACK):
            b = featurized(xb, LEAD + r, PACK, tap_b)
            gated_ref[r : r + PACK, lanes] = (b.astype(F32) * cot_head[r : r + PACK, lanes].astype(F32)).astype(BF16)
        b = featurized(xb, LEAD + taps, PACK, tap_b)
        for x, lead, head in ((xs, tail_a, first_head), (xt, tail_c, values_head)):
            x[:LEAD] = lead[:, lanes]
            x[LEAD:] = head[:, lanes].astype(F32)
        tile[...] = jnp.zeros_like(tile)
        tile[:1] = (b.astype(F32) * cot_next[:, lanes].astype(F32))[:1]
        tile[1:3] = featurized(xs, LEAD, PACK, tap_a).astype(F32)[:2]
        tile[3:5] = featurized(xt, LEAD, PACK, tap_c).astype(F32)[:2]
        tile[5:7] = cot_head[:PACK, lanes].astype(F32)[:2]
        gated_ref[taps:, lanes] = tile[...].astype(BF16)


def edges(part, stream, cot, tails, tap_rows, taps, width=8 * LANES):
    rows, channels = cot.shape
    all_steps = channels // width
    steps = all_steps // PARTS

    def column(which, height, at=0):
        return pl.BlockSpec((height, width), lambda j: (at, which * all_steps + part * steps + j))

    lead, last = (rows - taps) // PACK - 1, rows // taps - 1
    own = lambda j: (0, j)
    return pl.pallas_call(
        functools.partial(edge_kernel, width, taps),
        grid=(steps,),
        in_specs=[column(0, PACK, lead), column(0, taps, last), column(2, PACK, lead), column(2, taps, last)]
        + [column(0, PACK), column(2, PACK), column(1, taps), column(1, PACK, taps // PACK)]
        + [column(0, taps), column(0, PACK, taps // PACK)]
        + [column(w, LEAD) for w in range(3)]
        + [column(w, 3) for w in range(3)],
        out_specs=[pl.BlockSpec((taps, width), own), pl.BlockSpec((taps + PACK, width), own)],
        out_shape=[
            jax.ShapeDtypeStruct((taps, steps * width), BF16),
            jax.ShapeDtypeStruct((taps + PACK, steps * width), BF16),
        ],
        scratch_shapes=[
            pltpu.VMEM((PACK + taps, LANES), F32),
            pltpu.VMEM((LEAD + taps + PACK, LANES), F32),
            pltpu.VMEM((PACK + taps, LANES), F32),
            pltpu.VMEM((LEAD + PACK, LANES), F32),
            pltpu.VMEM((LEAD + PACK, LANES), F32),
            pltpu.VMEM((PACK, LANES), F32),
        ],
        compiler_params=pltpu.CompilerParams(vmem_limit_bytes=VMEM),
        cost_estimate=pl.CostEstimate(flops=10**7, bytes_accessed=4 * 10**6, transcendentals=0),
        name="edges",
    )(*[stream] * 8, cot, cot, *[tails] * 3, *[tap_rows] * 3)


def gates_kernel(width, rows, second_ref, tail_b, cot_ref, tb_ref, fb_ref, gated_ref, xb):
    for part in range(width // LANES):
        lanes = slice(part * LANES, (part + 1) * LANES)
        x = xb.at[part]
        (tap_b,) = taps_of((tb_ref,), lanes)
        x[:LEAD] = tail_b[:, lanes]
        x[LEAD:] = second_ref[:, lanes].astype(F32)
        for r in range(0, rows, PACK):
            b = featurized(x, LEAD + r, PACK, tap_b)
            fb_ref[r : r + PACK, lanes] = b
            gated_ref[r : r + PACK, lanes] = (b.astype(F32) * cot_ref[r : r + PACK, lanes].astype(F32)).astype(BF16)


def gates(stream, cot, tails, tap_rows, width=8 * LANES):
    rows, channels = cot.shape
    steps = channels // width

    def column(which, height):
        return pl.BlockSpec((height, width), lambda j: (0, which * steps + j))

    shape = jax.ShapeDtypeStruct((rows, channels), BF16)
    return pl.pallas_call(
        functools.partial(gates_kernel, width, rows),
        grid=(steps,),
        in_specs=[column(1, rows), column(1, LEAD), column(0, rows), column(1, 3)],
        out_specs=[column(0, rows)] * 2,
        out_shape=[shape, shape],
        scratch_shapes=[pltpu.VMEM((width // LANES, LEAD + rows, LANES), F32)],
        compiler_params=pltpu.CompilerParams(vmem_limit_bytes=VMEM),
        cost_estimate=pl.CostEstimate(flops=10**7, bytes_accessed=8 * 10**6, transcendentals=0),
        name="gates",
    )(stream, tails, cot, tap_rows)


def main_kernel(
    part, steps, width, rows, channels, taps, per_group, aliased, *refs
):
    (first_ref, second_ref, values_ref, cot_ref, before_ref, after_ref, fb_ref, gated_ref, tail_a, tail_c,
     ta_ref, tb_ref, tc_ref, ahead, behind) = refs[:15]
    result_ref, grad_ref, fgrad_ref, sgrad_ref = refs[15 + aliased : 19 + aliased]
    *buffers, wheels, held, sems = refs[19 + aliased :]
    step = pl.program_id(0)
    groups = LANES // per_group
    blocks = rows // BLOCK
    span = taps + BLOCK
    reach = taps + PACK
    inner_parts = width // LANES
    row = lax.broadcasted_iota(jnp.int32, (BLOCK, taps), 0)
    col = lax.broadcasted_iota(jnp.int32, (BLOCK, taps), 1)
    lane = lax.broadcasted_iota(jnp.int32, (BLOCK, LANES), 1)

    def diagonal_sums(at):
        for p in range(inner_parts):
            total = jnp.zeros((groups, taps), F32)
            for i in range(BLOCK):
                turned = wheels[pl.ds(p * groups * PITCH + i, groups, stride=PITCH), :]
                total = total + (pltpu.roll(turned, taps - i, 1) if i else turned)
            fgrad_ref[pl.ds(pl.multiple_of((at * inner_parts + p) * groups, groups), groups), :] = total

    diagonal_sums(jnp.maximum(step - 1, 0))

    def inner(p):
        lanes = slice(p * LANES, (p + 1) * LANES)
        xa, xc, fa, fc, mixed, gated, fga, fgb, fgc, masked, tile = (ref.at[p] for ref in buffers)
        tap_a, tap_b, tap_c = taps_of((ta_ref, tb_ref, tc_ref), lanes)
        for x, lead, own in ((xa, tail_a, first_ref), (xc, tail_c, values_ref)):
            x[:LEAD] = lead[:, lanes]
            x[LEAD:] = own[:, lanes].astype(F32)
        tile[:PACK] = after_ref[taps:, lanes].astype(F32)
        tile[PACK:] = jnp.zeros((PACK, LANES), F32)

        mixed[:taps] = before_ref[:, lanes]
        for r in range(0, rows, PACK):
            a = featurized(xa, LEAD + r, PACK, tap_a)
            c = featurized(xc, LEAD + r, PACK, tap_c)
            mixed[taps + r : taps + r + PACK] = (a.astype(F32) * c.astype(F32)).astype(BF16)
            fa[r : r + PACK] = a
            fc[r : r + PACK] = c
        mixed[taps + rows :] = (tile[1 : 1 + PACK] * tile[3 : 3 + PACK]).astype(BF16)
        gated[:rows] = gated_ref[:, lanes]
        gated[rows : rows + taps] = after_ref[:taps, lanes]
        gated[rows + taps :] = jnp.where(row[:PACK] == 0, tile[:PACK], 0.0).astype(BF16)

        top = p * groups * BLOCK

        toeplitz = ahead[top : top + groups * BLOCK, :span]
        for b in range(0, blocks, 2):
            product = jnp.dot(toeplitz, spans(mixed, b, 2, span), preferred_element_type=F32)
            for i in range(2):
                at = slice((b + i) * BLOCK, (b + i + 1) * BLOCK)
                hidden = pick_groups(product[:, i * LANES : (i + 1) * LANES], BLOCK, per_group)
                result_ref[at, lanes] = (fb_ref[at, lanes].astype(F32) * hidden).astype(BF16)
                fgb[at] = cot_ref[at, lanes].astype(F32) * hidden
        heads = [slice(top + g * BLOCK, top + g * BLOCK + PACK) for g in range(groups)]
        product = jnp.dot(
            jnp.concatenate([ahead[at, :reach] for at in heads], axis=0),
            mixed[rows : rows + reach],
            preferred_element_type=F32,
        )
        fgb[rows:] = tile[5 : 5 + PACK] * pick_groups(product, PACK, per_group)

        toeplitz = behind[top : top + groups * BLOCK, :span]
        for b in range(0, blocks, 2):
            product = jnp.dot(toeplitz, spans(gated, b, 2, span), preferred_element_type=F32)
            for i in range(2):
                at = slice((b + i) * BLOCK, (b + i + 1) * BLOCK)
                grad = pick_groups(product[:, i * LANES : (i + 1) * LANES], BLOCK, per_group)
                fga[at] = grad * fc[at].astype(F32)
                fgc[at] = grad * fa[at].astype(F32)
        product = jnp.dot(
            jnp.concatenate([behind[at, :reach] for at in heads], axis=0),
            gated[rows : rows + reach],
            preferred_element_type=F32,
        )
        grad = pick_groups(product, PACK, per_group)
        fga[rows:] = grad * tile[3 : 3 + PACK]
        fgc[rows:] = grad * tile[1 : 1 + PACK]

        for b in range(blocks):
            block = gated[b * BLOCK : (b + 1) * BLOCK].astype(F32)
            for g in range(groups):
                here = (lane >= g * per_group) & (lane < (g + 1) * per_group)
                masked[g * BLOCK : (g + 1) * BLOCK, b * LANES : (b + 1) * LANES] = jnp.where(here, block, 0.0).astype(
                    BF16
                )
        moment = lax.dot_general(
            masked[...], spans(mixed, 0, blocks, span), (((1,), (1,)), ((), ())), preferred_element_type=F32
        )
        for g in range(groups):
            at = slice(g * BLOCK, (g + 1) * BLOCK)
            later = jnp.concatenate([moment[at, taps:], jnp.zeros((BLOCK, taps - BLOCK), F32)], axis=1)
            start = (p * groups + g) * PITCH
            wheels[start : start + BLOCK] = jnp.where(col > row, moment[at, :taps], later)

        column = pl.multiple_of(step * width + p * LANES, LANES)
        for which, (fg, x, tap) in enumerate(((fga, xa, tap_a), (fgb, None, tap_b), (fgc, xc, tap_c))):
            sums = [jnp.zeros((8, LANES), F32) for _ in range(3)]
            for r in range(0, rows, PACK):
                near = [fg[pl.ds(r + s, PACK)] for s in range(3)]
                grad = tap[0] * near[0] + tap[1] * near[1] + tap[2] * near[2]
                held[r : r + PACK, pl.ds(which * steps * width + column, LANES)] = grad.astype(BF16)
                own = second_ref[r : r + PACK, lanes].astype(F32) if x is None else x[LEAD + r : LEAD + r + PACK]
                for s in range(3):
                    term = near[s] * own
                    sums[s] = sums[s] + (term[:8] + term[8:])
            for s in range(3):
                sgrad_ref[which, s : s + 1, lanes] = jnp.sum(sums[s], axis=0, keepdims=True)

    for p in range(inner_parts):
        inner(p)

    def copy(which, first, count):
        source = pl.ds(pl.multiple_of(which * steps * width + first, LANES), count)
        target = pl.ds(pl.multiple_of(which * channels + part * steps * width + first, LANES), count)
        return pltpu.make_async_copy(held.at[:, source], grad_ref.at[:, target], sems.at[which])

    for which in range(3):
        copy(which, step * width, width).start()

    @pl.when(step == steps - 1)
    def _():
        diagonal_sums(step)
        for which in range(3):
            copy(which, 0, steps * width).wait()


def main(part, stream, cot, before, after, fb, gated, tails, tap_rows, ahead, behind, earlier, taps, per_group, width=2 * LANES):
    rows, channels = cot.shape
    all_steps = channels // width
    steps = all_steps // PARTS
    groups = width // per_group
    offset = part * steps

    def column(which, height):
        return pl.BlockSpec((height, width), lambda j: (0, which * all_steps + offset + j))

    def own(height):
        return pl.BlockSpec((height, width), lambda j: (0, j))

    table = pl.BlockSpec((groups * BLOCK, 2 * taps), lambda j: (offset + j, 0))
    stacked = LANES // per_group * BLOCK
    inner = width // LANES
    outs = [jax.ShapeDtypeStruct((rows, channels), BF16), jax.ShapeDtypeStruct((rows, 3 * channels), BF16)]
    return pl.pallas_call(
        functools.partial(main_kernel, part, steps, width, rows, channels, taps, per_group, len(earlier)),
        grid=(steps,),
        in_specs=[column(w, rows) for w in range(3)]
        + [column(0, rows), own(taps), own(taps + PACK), column(0, rows), column(0, rows)]
        + [column(w, LEAD) for w in (0, 2)]
        + [column(w, 3) for w in range(3)]
        + [table, table]
        + [pl.BlockSpec(memory_space=pl.ANY)] * len(earlier),
        out_specs=[
            column(0, rows),
            pl.BlockSpec(memory_space=pl.ANY),
            pl.BlockSpec((steps * groups, taps), lambda j: (0, 0)),
            pl.BlockSpec((3, 3, width), lambda j: (0, 0, j)),
        ],
        out_shape=outs
        + [
            jax.ShapeDtypeStruct((steps * groups, taps), F32),
            jax.ShapeDtypeStruct((3, 3, steps * width), F32),
        ],
        scratch_shapes=[pltpu.VMEM((inner, LEAD + rows, LANES), F32)] * 2
        + [pltpu.VMEM((inner, rows, LANES), BF16)] * 2
        + [pltpu.VMEM((inner, taps + rows + PACK, LANES), BF16)] * 2
        + [pltpu.VMEM((inner, rows + PACK, LANES), F32)] * 3
        + [
            pltpu.VMEM((inner, stacked, rows // BLOCK * LANES), BF16),
            pltpu.VMEM((inner, 2 * PACK, LANES), F32),
            pltpu.VMEM((width // per_group * PITCH, taps), F32),
            pltpu.VMEM((rows, 3 * steps * width), BF16),
            pltpu.SemaphoreType.DMA((3,)),
        ],
        input_output_aliases={15 + i: i for i in range(len(earlier))},
        compiler_params=pltpu.CompilerParams(vmem_limit_bytes=MAIN_VMEM),
        cost_estimate=pl.CostEstimate(flops=10**10, bytes_accessed=2 * 10**7, transcendentals=0),
        name="hyena_main",
    )(*[stream] * 3, cot, before, after, fb, gated, *[tails] * 2, *[tap_rows] * 3, ahead, behind, *earlier)


def on_device(streams, cotangent, filters, short_taps):
    stream, cot = streams[0], cotangent[0]
    rows, channels = cot.shape
    own_groups, taps = filters.shape
    own_taps = short_taps.shape[1]
    device_count = lax.axis_size("fsdp") * lax.axis_size("ctx")
    group_count = own_groups * device_count
    per_group = channels // group_count

    tails = shifted(stream[rows - 2 :], "ctx", 1)
    tails = jnp.pad(tails.astype(F32), ((LEAD - 2, 0), (0, 0)))

    padding = -own_taps % LANES
    own = jnp.concatenate(
        [filters.reshape(1, -1), jnp.pad(short_taps, ((0, 0), (0, padding))).reshape(1, -1)], axis=1
    )
    whole = lax.all_to_all(
        jnp.broadcast_to(own, (device_count, own.shape[1])), ("fsdp", "ctx"), 0, 0, tiled=True
    )
    whole_filters = whole[:, : own_groups * taps].reshape(group_count, taps)
    whole_taps = whole[:, own_groups * taps :].reshape(device_count, 3, own_taps + padding)[:, :, :own_taps]
    whole_taps = whole_taps.transpose(1, 0, 2).reshape(3, device_count * own_taps)

    halos = []
    for part in range(PARTS):
        mixed_tail, gated_head = edges(part, stream, cot, tails, whole_taps, taps)
        halos.append((shifted(mixed_tail, "ctx", 1), shifted(gated_head, "ctx", -1)))
    ahead, behind = toeplitz_blocks(whole_filters)
    fb, gated = gates(stream, cot, tails, whole_taps)
    earlier, filter_parts, short_parts = (), [], []
    for part in range(PARTS):
        result, stream_grad, filter_part, short_part = main(
            part, stream, cot, *halos[part], fb, gated, tails, whole_taps, ahead, behind, earlier, taps, per_group
        )
        earlier = (result, stream_grad)
        filter_parts.append(filter_part)
        short_parts.append(short_part)

    filter_part = jnp.concatenate(filter_parts, axis=0).reshape(device_count, own_groups * taps)
    short_part = jnp.concatenate(short_parts, axis=2)
    short_part = short_part.transpose(1, 0, 2).reshape(3, device_count, own_taps).transpose(1, 0, 2)
    short_part = jnp.pad(short_part, ((0, 0), (0, 0), (0, padding))).reshape(device_count, -1)
    terms = lax.all_to_all(
        jnp.concatenate([filter_part, short_part], axis=1), ("fsdp", "ctx"), 0, 0, tiled=True
    )
    factor = 1.0 / math.sqrt(device_count * rows)
    total = jnp.sum(terms, axis=0) * factor
    filter_grad = jnp.roll(total[: own_groups * taps].reshape(own_groups, taps)[:, ::-1], 1, axis=1)
    short_grad = total[own_groups * taps :].reshape(3, own_taps + padding)[:, :own_taps]
    return (result[None], stream_grad[None], filter_grad, short_grad)


def solution(mesh):
    in_specs = (
        P("fsdp", "ctx", None),
        P("fsdp", "ctx", None),
        P(("fsdp", "ctx"), None),
        P(None, ("fsdp", "ctx")),
    )
    out_specs = (
        P("fsdp", "ctx", None),
        P("fsdp", "ctx", None),
        P(("fsdp", "ctx"), None),
        P(None, ("fsdp", "ctx")),
    )
    return jax.shard_map(
        on_device, mesh=mesh, in_specs=in_specs, out_specs=out_specs, check_vma=False
    )
```

```python
import functools
import math

import jax
import jax.numpy as jnp
import numpy as np
from jax import lax
from jax.experimental import pallas as pl
from jax.experimental.pallas import tpu as pltpu
from jax.sharding import PartitionSpec as P

F32, BF16 = jnp.float32, jnp.bfloat16
LANES = 128
PACK = 16
BLOCK = 32
PITCH = BLOCK + 8
LEAD = 8
PARTS = 1
VMEM = 24 * 1024 * 1024
EDGE_VMEM = 61 * 1024 * 1024
MAIN_VMEM = 46 * 1024 * 1024


def shifted(value, axis, by):
    length = lax.axis_size(axis)
    pairs = [(i, i + by) for i in range(length) if 0 <= i + by < length]
    return lax.ppermute(value, axis, pairs)


def pick_groups(product, block, per_group):
    lane = lax.broadcasted_iota(jnp.int32, (block, LANES), 1)
    total = product[:block]
    for g in range(1, LANES // per_group):
        total = jnp.where(lane >= g * per_group, product[g * block : (g + 1) * block], total)
    return total


def featurized(x, at, count, tap):
    return (
        tap[0] * x[pl.ds(at, count)] + tap[1] * x[pl.ds(at - 1, count)] + tap[2] * x[pl.ds(at - 2, count)]
    ).astype(BF16)


def spans(ref, first, count, width):
    return jnp.concatenate([ref[(first + i) * BLOCK : (first + i) * BLOCK + width] for i in range(count)], axis=1)


def taps_of(refs, lanes):
    return [[ref[s : s + 1, lanes] for s in range(3)] for ref in refs]


def toeplitz_kernel(taps, filters_ref, turn_ref, ahead_ref, behind_ref):
    row = lax.broadcasted_iota(jnp.int32, (BLOCK, taps), 0)
    col = lax.broadcasted_iota(jnp.int32, (BLOCK, taps), 1)
    zero = jnp.zeros((BLOCK, taps), F32)
    straight = filters_ref[...]
    reverse = jnp.dot(straight.astype(BF16), turn_ref[...], preferred_element_type=F32)
    for g in range(straight.shape[0]):
        at = slice(g * BLOCK, (g + 1) * BLOCK)
        wheel = pltpu.roll(jnp.broadcast_to(reverse[g : g + 1], (BLOCK, taps)), 0, 1, stride=1, stride_axis=0)
        ahead_ref[at, :taps] = jnp.where(col > row, wheel, zero).astype(BF16)
        ahead_ref[at, taps:] = jnp.where(col > row, zero, wheel).astype(BF16)
        wheel = pltpu.roll(jnp.broadcast_to(straight[g : g + 1], (BLOCK, taps)), 0, 1, stride=1, stride_axis=0)
        behind_ref[at, :taps] = jnp.where(col >= row, wheel, zero).astype(BF16)
        behind_ref[at, taps:] = jnp.where(col >= row, zero, wheel).astype(BF16)


def toeplitz_blocks(filters, batch=64):
    group_count, taps = filters.shape
    index = np.arange(taps)
    turn = jnp.asarray(index[:, None] == (-index[None, :]) % taps, BF16)
    out = pl.BlockSpec((batch * BLOCK, 2 * taps), lambda j: (j, 0))
    shape = jax.ShapeDtypeStruct((group_count * BLOCK, 2 * taps), BF16)
    return pl.pallas_call(
        functools.partial(toeplitz_kernel, taps),
        grid=(group_count // batch,),
        in_specs=[pl.BlockSpec((batch, taps), lambda j: (j, 0)), pl.BlockSpec((taps, taps), lambda j: (0, 0))],
        out_specs=[out, out],
        out_shape=[shape, shape],
        compiler_params=pltpu.CompilerParams(vmem_limit_bytes=VMEM),
        cost_estimate=pl.CostEstimate(flops=10**9, bytes_accessed=10**7, transcendentals=0),
        name="toeplitz_blocks",
    )(filters, turn)


def edge_kernel(
    width, taps,
    first_lead, first_tail, values_lead, values_tail, first_head, values_head, second_head, second_next,
    cot_head, cot_next, tail_a, tail_b, tail_c, ta_ref, tb_ref, tc_ref,
    mixed_ref, gated_ref,
    xa, xb, xc, xs, xt, tile,
):
    for part in range(width // LANES):
        lanes = slice(part * LANES, (part + 1) * LANES)
        tap_a, tap_b, tap_c = taps_of((ta_ref, tb_ref, tc_ref), lanes)
        for x, lead, tail in ((xa, first_lead, first_tail), (xc, values_lead, values_tail)):
            x[:PACK] = lead[:, lanes].astype(F32)
            x[PACK:] = tail[:, lanes].astype(F32)
        for r in range(0, taps, PACK):
            a = featurized(xa, PACK + r, PACK, tap_a)
            c = featurized(xc, PACK + r, PACK, tap_c)
            mixed_ref[r : r + PACK, lanes] = (a.astype(F32) * c.astype(F32)).astype(BF16)
        xb[:LEAD] = tail_b[:, lanes]
        xb[LEAD : LEAD + taps] = second_head[:, lanes].astype(F32)
        xb[LEAD + taps :] = second_next[:, lanes].astype(F32)
        for r in range(0, taps, PACK):
            b = featurized(xb, LEAD + r, PACK, tap_b)
            gated_ref[r : r + PACK, lanes] = (b.astype(F32) * cot_head[r : r + PACK, lanes].astype(F32)).astype(BF16)
        b = featurized(xb, LEAD + taps, PACK, tap_b)
        for x, lead, head in ((xs, tail_a, first_head), (xt, tail_c, values_head)):
            x[:LEAD] = lead[:, lanes]
            x[LEAD:] = head[:, lanes].astype(F32)
        tile[...] = jnp.zeros_like(tile)
        tile[:1] = (b.astype(F32) * cot_next[:, lanes].astype(F32))[:1]
        tile[1:3] = featurized(xs, LEAD, PACK, tap_a).astype(F32)[:2]
        tile[3:5] = featurized(xt, LEAD, PACK, tap_c).astype(F32)[:2]
        tile[5:7] = cot_head[:PACK, lanes].astype(F32)[:2]
        gated_ref[taps:, lanes] = tile[...].astype(BF16)


def edges(part, stream, cot, tails, tap_rows, taps, width=8 * LANES):
    rows, channels = cot.shape
    all_steps = channels // width
    steps = all_steps // PARTS

    def column(which, height, at=0):
        return pl.BlockSpec((height, width), lambda j: (at, which * all_steps + part * steps + j))

    lead, last = (rows - taps) // PACK - 1, rows // taps - 1
    own = lambda j: (0, j)
    return pl.pallas_call(
        functools.partial(edge_kernel, width, taps),
        grid=(steps,),
        in_specs=[column(0, PACK, lead), column(0, taps, last), column(2, PACK, lead), column(2, taps, last)]
        + [column(0, PACK), column(2, PACK), column(1, taps), column(1, PACK, taps // PACK)]
        + [column(0, taps), column(0, PACK, taps // PACK)]
        + [column(w, LEAD) for w in range(3)]
        + [column(w, 3) for w in range(3)],
        out_specs=[pl.BlockSpec((taps, width), own), pl.BlockSpec((taps + PACK, width), own)],
        out_shape=[
            jax.ShapeDtypeStruct((taps, steps * width), BF16),
            jax.ShapeDtypeStruct((taps + PACK, steps * width), BF16),
        ],
        scratch_shapes=[
            pltpu.VMEM((PACK + taps, LANES), F32),
            pltpu.VMEM((LEAD + taps + PACK, LANES), F32),
            pltpu.VMEM((PACK + taps, LANES), F32),
            pltpu.VMEM((LEAD + PACK, LANES), F32),
            pltpu.VMEM((LEAD + PACK, LANES), F32),
            pltpu.VMEM((PACK, LANES), F32),
        ],
        compiler_params=pltpu.CompilerParams(vmem_limit_bytes=EDGE_VMEM),
        cost_estimate=pl.CostEstimate(flops=10**7, bytes_accessed=4 * 10**6, transcendentals=0),
        name="edges",
    )(*[stream] * 8, cot, cot, *[tails] * 3, *[tap_rows] * 3)


def gates_kernel(width, rows, second_ref, tail_b, cot_ref, tb_ref, fb_ref, gated_ref, xb):
    for part in range(width // LANES):
        lanes = slice(part * LANES, (part + 1) * LANES)
        x = xb.at[part]
        (tap_b,) = taps_of((tb_ref,), lanes)
        x[:LEAD] = tail_b[:, lanes]
        x[LEAD:] = second_ref[:, lanes].astype(F32)
        for r in range(0, rows, PACK):
            b = featurized(x, LEAD + r, PACK, tap_b)
            fb_ref[r : r + PACK, lanes] = b
            gated_ref[r : r + PACK, lanes] = (b.astype(F32) * cot_ref[r : r + PACK, lanes].astype(F32)).astype(BF16)


def gates(stream, cot, tails, tap_rows, width=8 * LANES):
    rows, channels = cot.shape
    steps = channels // width

    def column(which, height):
        return pl.BlockSpec((height, width), lambda j: (0, which * steps + j))

    shape = jax.ShapeDtypeStruct((rows, channels), BF16)
    return pl.pallas_call(
        functools.partial(gates_kernel, width, rows),
        grid=(steps,),
        in_specs=[column(1, rows), column(1, LEAD), column(0, rows), column(1, 3)],
        out_specs=[column(0, rows)] * 2,
        out_shape=[shape, shape],
        scratch_shapes=[pltpu.VMEM((width // LANES, LEAD + rows, LANES), F32)],
        compiler_params=pltpu.CompilerParams(vmem_limit_bytes=VMEM),
        cost_estimate=pl.CostEstimate(flops=10**7, bytes_accessed=8 * 10**6, transcendentals=0),
        name="gates",
    )(stream, tails, cot, tap_rows)


def main_kernel(
    part, steps, width, rows, channels, taps, per_group, aliased, *refs
):
    (first_ref, second_ref, values_ref, cot_ref, before_ref, after_ref, fb_ref, gated_ref, tail_a, tail_c,
     ta_ref, tb_ref, tc_ref, ahead, behind) = refs[:15]
    result_ref, grad_ref, fgrad_ref, sgrad_ref = refs[15 + aliased : 19 + aliased]
    *buffers, wheels, held, sems = refs[19 + aliased :]
    step = pl.program_id(0)
    groups = LANES // per_group
    blocks = rows // BLOCK
    span = taps + BLOCK
    reach = taps + PACK
    inner_parts = width // LANES
    row = lax.broadcasted_iota(jnp.int32, (BLOCK, taps), 0)
    col = lax.broadcasted_iota(jnp.int32, (BLOCK, taps), 1)
    lane = lax.broadcasted_iota(jnp.int32, (BLOCK, LANES), 1)

    def diagonal_sums(at):
        for p in range(inner_parts):
            total = jnp.zeros((groups, taps), F32)
            for i in range(BLOCK):
                turned = wheels[pl.ds(p * groups * PITCH + i, groups, stride=PITCH), :]
                total = total + (pltpu.roll(turned, taps - i, 1) if i else turned)
            fgrad_ref[pl.ds(pl.multiple_of((at * inner_parts + p) * groups, groups), groups), :] = total

    diagonal_sums(jnp.maximum(step - 1, 0))

    def inner(p):
        lanes = slice(p * LANES, (p + 1) * LANES)
        xa, xc, fa, fc, mixed, gated, fga, fgb, fgc, masked, tile = (ref.at[p] for ref in buffers)
        tap_a, tap_b, tap_c = taps_of((ta_ref, tb_ref, tc_ref), lanes)
        for x, lead, own in ((xa, tail_a, first_ref), (xc, tail_c, values_ref)):
            x[:LEAD] = lead[:, lanes]
            x[LEAD:] = own[:, lanes].astype(F32)
        tile[:PACK] = after_ref[taps:, lanes].astype(F32)
        tile[PACK:] = jnp.zeros((PACK, LANES), F32)

        mixed[:taps] = before_ref[:, lanes]
        for r in range(0, rows, PACK):
            a = featurized(xa, LEAD + r, PACK, tap_a)
            c = featurized(xc, LEAD + r, PACK, tap_c)
            mixed[taps + r : taps + r + PACK] = (a.astype(F32) * c.astype(F32)).astype(BF16)
            fa[r : r + PACK] = a
            fc[r : r + PACK] = c
        mixed[taps + rows :] = (tile[1 : 1 + PACK] * tile[3 : 3 + PACK]).astype(BF16)
        gated[:rows] = gated_ref[:, lanes]
        gated[rows : rows + taps] = after_ref[:taps, lanes]
        gated[rows + taps :] = jnp.where(row[:PACK] == 0, tile[:PACK], 0.0).astype(BF16)

        top = p * groups * BLOCK

        toeplitz = ahead[top : top + groups * BLOCK, :span]
        for b in range(0, blocks, 2):
            product = jnp.dot(toeplitz, spans(mixed, b, 2, span), preferred_element_type=F32)
            for i in range(2):
                at = slice((b + i) * BLOCK, (b + i + 1) * BLOCK)
                hidden = pick_groups(product[:, i * LANES : (i + 1) * LANES], BLOCK, per_group)
                result_ref[at, lanes] = (fb_ref[at, lanes].astype(F32) * hidden).astype(BF16)
                fgb[at] = cot_ref[at, lanes].astype(F32) * hidden
        heads = [slice(top + g * BLOCK, top + g * BLOCK + PACK) for g in range(groups)]
        product = jnp.dot(
            jnp.concatenate([ahead[at, :reach] for at in heads], axis=0),
            mixed[rows : rows + reach],
            preferred_element_type=F32,
        )
        fgb[rows:] = tile[5 : 5 + PACK] * pick_groups(product, PACK, per_group)

        toeplitz = behind[top : top + groups * BLOCK, :span]
        for b in range(0, blocks, 2):
            product = jnp.dot(toeplitz, spans(gated, b, 2, span), preferred_element_type=F32)
            for i in range(2):
                at = slice((b + i) * BLOCK, (b + i + 1) * BLOCK)
                grad = pick_groups(product[:, i * LANES : (i + 1) * LANES], BLOCK, per_group)
                fga[at] = grad * fc[at].astype(F32)
                fgc[at] = grad * fa[at].astype(F32)
        product = jnp.dot(
            jnp.concatenate([behind[at, :reach] for at in heads], axis=0),
            gated[rows : rows + reach],
            preferred_element_type=F32,
        )
        grad = pick_groups(product, PACK, per_group)
        fga[rows:] = grad * tile[3 : 3 + PACK]
        fgc[rows:] = grad * tile[1 : 1 + PACK]

        for b in range(blocks):
            block = gated[b * BLOCK : (b + 1) * BLOCK].astype(F32)
            for g in range(groups):
                here = (lane >= g * per_group) & (lane < (g + 1) * per_group)
                masked[g * BLOCK : (g + 1) * BLOCK, b * LANES : (b + 1) * LANES] = jnp.where(here, block, 0.0).astype(
                    BF16
                )
        moment = lax.dot_general(
            masked[...], spans(mixed, 0, blocks, span), (((1,), (1,)), ((), ())), preferred_element_type=F32
        )
        for g in range(groups):
            at = slice(g * BLOCK, (g + 1) * BLOCK)
            later = jnp.concatenate([moment[at, taps:], jnp.zeros((BLOCK, taps - BLOCK), F32)], axis=1)
            start = (p * groups + g) * PITCH
            wheels[start : start + BLOCK] = jnp.where(col > row, moment[at, :taps], later)

        column = pl.multiple_of(step * width + p * LANES, LANES)
        for which, (fg, x, tap) in enumerate(((fga, xa, tap_a), (fgb, None, tap_b), (fgc, xc, tap_c))):
            sums = [jnp.zeros((8, LANES), F32) for _ in range(3)]
            for r in range(0, rows, PACK):
                near = [fg[pl.ds(r + s, PACK)] for s in range(3)]
                grad = tap[0] * near[0] + tap[1] * near[1] + tap[2] * near[2]
                held[r : r + PACK, pl.ds(which * steps * width + column, LANES)] = grad.astype(BF16)
                own = second_ref[r : r + PACK, lanes].astype(F32) if x is None else x[LEAD + r : LEAD + r + PACK]
                for s in range(3):
                    term = near[s] * own
                    sums[s] = sums[s] + (term[:8] + term[8:])
            for s in range(3):
                sgrad_ref[which, s : s + 1, lanes] = jnp.sum(sums[s], axis=0, keepdims=True)

    for p in range(inner_parts):
        inner(p)

    def copy(which, first, count):
        source = pl.ds(pl.multiple_of(which * steps * width + first, LANES), count)
        target = pl.ds(pl.multiple_of(which * channels + part * steps * width + first, LANES), count)
        return pltpu.make_async_copy(held.at[:, source], grad_ref.at[:, target], sems.at[which])

    for which in range(3):
        copy(which, step * width, width).start()

    @pl.when(step == steps - 1)
    def _():
        diagonal_sums(step)
        for which in range(3):
            copy(which, 0, steps * width).wait()


def main(part, stream, cot, before, after, fb, gated, tails, tap_rows, ahead, behind, earlier, taps, per_group, width=2 * LANES):
    rows, channels = cot.shape
    all_steps = channels // width
    steps = all_steps // PARTS
    groups = width // per_group
    offset = part * steps

    def column(which, height):
        return pl.BlockSpec((height, width), lambda j: (0, which * all_steps + offset + j))

    def own(height):
        return pl.BlockSpec((height, width), lambda j: (0, j))

    table = pl.BlockSpec((groups * BLOCK, 2 * taps), lambda j: (offset + j, 0))
    stacked = LANES // per_group * BLOCK
    inner = width // LANES
    outs = [jax.ShapeDtypeStruct((rows, channels), BF16), jax.ShapeDtypeStruct((rows, 3 * channels), BF16)]
    return pl.pallas_call(
        functools.partial(main_kernel, part, steps, width, rows, channels, taps, per_group, len(earlier)),
        grid=(steps,),
        in_specs=[column(w, rows) for w in range(3)]
        + [column(0, rows), own(taps), own(taps + PACK), column(0, rows), column(0, rows)]
        + [column(w, LEAD) for w in (0, 2)]
        + [column(w, 3) for w in range(3)]
        + [table, table]
        + [pl.BlockSpec(memory_space=pl.ANY)] * len(earlier),
        out_specs=[
            column(0, rows),
            pl.BlockSpec(memory_space=pl.ANY),
            pl.BlockSpec((steps * groups, taps), lambda j: (0, 0)),
            pl.BlockSpec((3, 3, width), lambda j: (0, 0, j)),
        ],
        out_shape=outs
        + [
            jax.ShapeDtypeStruct((steps * groups, taps), F32),
            jax.ShapeDtypeStruct((3, 3, steps * width), F32),
        ],
        scratch_shapes=[pltpu.VMEM((inner, LEAD + rows, LANES), F32)] * 2
        + [pltpu.VMEM((inner, rows, LANES), BF16)] * 2
        + [pltpu.VMEM((inner, taps + rows + PACK, LANES), BF16)] * 2
        + [pltpu.VMEM((inner, rows + PACK, LANES), F32)] * 3
        + [
            pltpu.VMEM((inner, stacked, rows // BLOCK * LANES), BF16),
            pltpu.VMEM((inner, 2 * PACK, LANES), F32),
            pltpu.VMEM((width // per_group * PITCH, taps), F32),
            pltpu.VMEM((rows, 3 * steps * width), BF16),
            pltpu.SemaphoreType.DMA((3,)),
        ],
        input_output_aliases={15 + i: i for i in range(len(earlier))},
        compiler_params=pltpu.CompilerParams(vmem_limit_bytes=MAIN_VMEM),
        cost_estimate=pl.CostEstimate(flops=10**10, bytes_accessed=2 * 10**7, transcendentals=0),
        name="hyena_main",
    )(*[stream] * 3, cot, before, after, fb, gated, *[tails] * 2, *[tap_rows] * 3, ahead, behind, *earlier)


def on_device(streams, cotangent, filters, short_taps):
    stream, cot = streams[0], cotangent[0]
    rows, channels = cot.shape
    own_groups, taps = filters.shape
    own_taps = short_taps.shape[1]
    device_count = lax.axis_size("fsdp") * lax.axis_size("ctx")
    group_count = own_groups * device_count
    per_group = channels // group_count

    tails = shifted(stream[rows - 2 :], "ctx", 1)
    tails = jnp.pad(tails.astype(F32), ((LEAD - 2, 0), (0, 0)))

    padding = -own_taps % LANES
    own = jnp.concatenate(
        [filters.reshape(1, -1), jnp.pad(short_taps, ((0, 0), (0, padding))).reshape(1, -1)], axis=1
    )
    whole = lax.all_to_all(
        jnp.broadcast_to(own, (device_count, own.shape[1])), ("fsdp", "ctx"), 0, 0, tiled=True
    )
    whole_filters = whole[:, : own_groups * taps].reshape(group_count, taps)
    whole_taps = whole[:, own_groups * taps :].reshape(device_count, 3, own_taps + padding)[:, :, :own_taps]
    whole_taps = whole_taps.transpose(1, 0, 2).reshape(3, device_count * own_taps)

    halos = []
    for part in range(PARTS):
        mixed_tail, gated_head = edges(part, stream, cot, tails, whole_taps, taps)
        halos.append((shifted(mixed_tail, "ctx", 1), shifted(gated_head, "ctx", -1)))
    ahead, behind = toeplitz_blocks(whole_filters)
    fb, gated = gates(stream, cot, tails, whole_taps)
    earlier, filter_parts, short_parts = (), [], []
    for part in range(PARTS):
        result, stream_grad, filter_part, short_part = main(
            part, stream, cot, *halos[part], fb, gated, tails, whole_taps, ahead, behind, earlier, taps, per_group
        )
        earlier = (result, stream_grad)
        filter_parts.append(filter_part)
        short_parts.append(short_part)

    filter_part = jnp.concatenate(filter_parts, axis=0).reshape(device_count, own_groups * taps)
    short_part = jnp.concatenate(short_parts, axis=2)
    short_part = short_part.transpose(1, 0, 2).reshape(3, device_count, own_taps).transpose(1, 0, 2)
    short_part = jnp.pad(short_part, ((0, 0), (0, 0), (0, padding))).reshape(device_count, -1)
    terms = lax.all_to_all(
        jnp.concatenate([filter_part, short_part], axis=1), ("fsdp", "ctx"), 0, 0, tiled=True
    )
    factor = 1.0 / math.sqrt(device_count * rows)
    total = jnp.sum(terms, axis=0) * factor
    filter_grad = jnp.roll(total[: own_groups * taps].reshape(own_groups, taps)[:, ::-1], 1, axis=1)
    short_grad = total[own_groups * taps :].reshape(3, own_taps + padding)[:, :own_taps]
    return (result[None], stream_grad[None], filter_grad, short_grad)


def solution(mesh):
    in_specs = (
        P("fsdp", "ctx", None),
        P("fsdp", "ctx", None),
        P(("fsdp", "ctx"), None),
        P(None, ("fsdp", "ctx")),
    )
    out_specs = (
        P("fsdp", "ctx", None),
        P("fsdp", "ctx", None),
        P(("fsdp", "ctx"), None),
        P(None, ("fsdp", "ctx")),
    )
    return jax.shard_map(
        on_device, mesh=mesh, in_specs=in_specs, out_specs=out_specs, check_vma=False
    )
```
